32 devices in a mesh: grp: 2 (over y), src: 16 (over z, x, core).
Axes of the slice: x: 2, y: 2, z: 4, core: 2. Of those that a mesh axis runs over, the one named last changes fastest.
Arguments:
- kernel: bfloat16 [2560, 256, 256], P(('grp', 'src')), parts along dimension 0, may hold values from 1.953125e-07 to 0.0146484375
- pair_source: int32 [2560], P(('grp', 'src')), parts along dimension 0, may hold values from 0 to 15, as said below
- pair_target: int32 [2560], P(('grp', 'src')), parts along dimension 0, may hold values from 0 to 21, as said below
- source_cells: int32 [512], P(('grp', 'src')), parts along dimension 0, may hold values from 129 to 256
- target_cells: int32 [512], P(('grp', 'src')), parts along dimension 0, may hold values from 129 to 256
- source_hist: bfloat16 [64, 131072], P(None, ('grp', 'src')), parts along dimension 1, may hold values from 0.049804688 to 2
- target_hist: bfloat16 [64, 131072], P(None, ('grp', 'src')), parts along dimension 1, may hold values from 0.05 to 2
- warm_start: bfloat16 [64, 131072], P(None, ('grp', 'src')), parts along dimension 1, may hold values from 0.5 to 2
Outputs:
- target_scaling: bfloat16 [64, 131072], P(None, ('grp', 'src')), parts along dimension 1
- row_marginal: bfloat16 [64, 131072], P(None, ('grp', 'src')), parts along dimension 1
The draws below stay inside these ranges and needn't reach their ends.
There are 2 independent parts, one for each index of `grp`. The reference program is written for one: setup_inputs(seed, part) draws one part's arguments, and reference() takes and returns one part's arrays. A program takes and returns all parts, laid end to end along the dimension named above; each array names one. Nothing has to cross between parts.
Inputs may be any that keep to these rules, and one draw needn't show every extreme that they name: `pair_source`: on each device every source block has 1 to 7 pairs with distinct target positions, within 3 of its own index plus 3, always including that aligned position; on every device some source block has exactly 7 pairs. `pair_target`: window position w of a pair with source block b lies between b and b + 6.
All inputs are finite; a program needn't handle non-finite values.
Results may differ from the reference program's by a relative error of at most 0.008.
Values may be sent and summed in bfloat16 or wider, within the bound.
A program may use at most 64 MiB of HBM per device.

```python
import math
import jax
import jax.numpy as jnp
from jax import lax

H = 64
BLK = 256
SB_DEV = 16
RIM = 3
ITERS = 2
PAIRS_DEV = 80
PAIRS = 1280
NBS = 256
NS = 65536
N_SRC = 16


def device_pairs(key):
    first_key, second_key, third_key, fourth_key = jax.random.split(key, 4)
    reach_count = 2 * RIM
    extras = PAIRS_DEV - SB_DEV
    scores = jax.random.permutation(first_key, SB_DEV * reach_count).astype(jnp.int32)
    full_block = jax.random.randint(second_key, (), 0, SB_DEV, dtype=jnp.int32)
    slot_block = jnp.arange(SB_DEV * reach_count, dtype=jnp.int32) // reach_count
    scores = jnp.where(slot_block == full_block, scores + SB_DEV * reach_count, scores)
    chosen = jnp.argsort(-scores, stable=True)[:extras].astype(jnp.int32)
    others = jnp.concatenate([jnp.arange(-RIM, 0, dtype=jnp.int32), jnp.arange(1, RIM + 1, dtype=jnp.int32)])
    shuffles = jax.vmap(lambda sub_key: jax.random.permutation(sub_key, others))(jax.random.split(third_key, SB_DEV))
    chosen_block = chosen // reach_count
    chosen_slot = chosen % reach_count
    offsets = shuffles[chosen_block, chosen_slot]
    aligned = jnp.arange(SB_DEV, dtype=jnp.int32)
    sources = jnp.concatenate([aligned, chosen_block])
    targets = jnp.concatenate([aligned + RIM, chosen_block + RIM + offsets])
    shuffle = jax.random.permutation(fourth_key, PAIRS_DEV)
    return (sources[shuffle].astype(jnp.int32), targets[shuffle].astype(jnp.int32))


def pair_layout(key):
    device_keys = jax.random.split(key, N_SRC)
    sources, targets = jax.vmap(device_pairs)(device_keys)
    return (sources.reshape(-1), targets.reshape(-1))


def draw_pair_source(key, part):
    return pair_layout(key)[0]


def draw_pair_target(key, part):
    return pair_layout(key)[1]


def draw_kernel(key, part):
    targets = pair_layout(key)[1]
    key = jax.random.fold_in(key, 5)
    column_key, rough_key = jax.random.split(key)
    column_scale = jnp.exp(jax.random.uniform(column_key, (NBS + 2 * RIM, BLK), jnp.float32, math.log(0.4), math.log(2.5)))
    device_of = jnp.arange(PAIRS, dtype=jnp.int32) // PAIRS_DEV
    global_block = (device_of * SB_DEV + targets).astype(jnp.int32)
    columns = jnp.take(column_scale, global_block, axis=0)
    slots = jnp.arange(BLK, dtype=jnp.float32)
    envelope = jnp.exp(-8.0 * jnp.abs(slots[:, None] - slots[None, :]) / BLK)
    rough = jnp.exp(jax.random.uniform(rough_key, (PAIRS, BLK, BLK), jnp.float32, math.log(0.5), math.log(2.0)))
    values = 0.75 / BLK * envelope[None, :, :] * columns[:, None, :] * rough
    return values.astype(jnp.bfloat16)


def draw_target_hist(key, part):
    key = jax.random.fold_in(key, 11)
    shared_key, block_key, rough_key = jax.random.split(key, 3)
    pieces = 2
    shared = jnp.exp(jax.random.uniform(shared_key, (H, 1, pieces), jnp.float32, math.log(0.1), 0.0))
    local = jnp.exp(jax.random.uniform(block_key, (H, NBS, pieces), jnp.float32, 0.0, math.log(2.0)))
    level = jnp.repeat(shared * local, BLK // pieces, axis=2)
    rough = jnp.exp(jax.random.uniform(rough_key, (H, NBS, BLK), jnp.float32, math.log(0.5), 0.0))
    return (level * rough).reshape(H, NS).astype(jnp.bfloat16)


def touch_ends(entries, stream_key, low, top_value):
    shape = entries.shape
    place = [jax.random.randint(jax.random.fold_in(stream_key, axis), (), 0, shape[axis]) for axis in range(len(shape))]
    entries = entries.at[tuple(place)].set(low)
    longest = shape.index(max(shape))
    place[longest] = (place[longest] + 1) % shape[longest]
    return entries.at[tuple(place)].set(top_value)


def block_levels(key, dims, cuts, smallest, largest):
    factor_of = 1.0
    for dim, parts in cuts:
        steps = jax.random.uniform(jax.random.fold_in(jax.random.fold_in(key, 6), dim), (parts,), jnp.float32, smallest / len(cuts), largest / len(cuts))
        factor_of = factor_of * jnp.repeat(jnp.exp(steps), dims[dim] // parts).reshape((-1,) + (1,) * (len(dims) - 1 - dim))
    return factor_of


def setup_inputs(seed: int = 0, part: int = 0) -> dict:
    keys = jax.random.split(jax.random.key(seed), 9)
    own_keys = jax.random.split(jax.random.fold_in(keys[8], part), 9)
    return {
        "kernel": draw_kernel(jax.random.fold_in(jax.random.fold_in(keys[8], part), 71), part),
        "pair_source": draw_pair_source(jax.random.fold_in(jax.random.fold_in(keys[8], part), 71), part),
        "pair_target": draw_pair_target(jax.random.fold_in(jax.random.fold_in(keys[8], part), 71), part),
        "source_cells": touch_ends(jax.random.randint(own_keys[3], (NBS,), BLK // 2 + 1, BLK + 1), jax.random.fold_in(own_keys[3], 1), BLK // 2 + 1, BLK).astype(jnp.int32),
        "target_cells": touch_ends(jax.random.randint(own_keys[4], (NBS,), BLK // 2 + 1, BLK + 1), jax.random.fold_in(own_keys[4], 1), BLK // 2 + 1, BLK).astype(jnp.int32),
        "source_hist": jnp.clip(jnp.exp(math.log(2.0) - 3.6927934 * jax.random.uniform(own_keys[5], (H, NS), jnp.float32) ** block_levels(own_keys[5], (H, NS), ((1, 16),), -0.2, 0.2)), 0.049804688, 2.0).astype(jnp.bfloat16),
        "target_hist": draw_target_hist(jax.random.fold_in(jax.random.fold_in(keys[8], part), 71), part),
        "warm_start": jnp.clip(jnp.exp(math.log(2.0) - 1.3862944 * jax.random.uniform(own_keys[7], (H, NS), jnp.float32) ** block_levels(own_keys[7], (H, NS), ((1, 16),), -0.2, 0.2)), 0.5, 2.0).astype(jnp.bfloat16),
    }


def reference(kernel, pair_source, pair_target, source_cells, target_cells, source_hist, target_hist, warm_start):
    window_len = SB_DEV + 2 * RIM
    slot_ids = jnp.arange(BLK, dtype=jnp.int32)
    source_live = slot_ids[None, :] < source_cells[:, None]
    target_live = slot_ids[None, :] < target_cells[:, None]

    def to_device(field, live):
        blocks = jnp.where(live[None], field.astype(jnp.float32).reshape(H, NBS, BLK), 0.0)
        return blocks.reshape(H, N_SRC, SB_DEV, BLK).transpose(1, 0, 2, 3)

    def from_device(field):
        return field.transpose(1, 0, 2, 3).reshape(H, NS)

    source_mass = to_device(source_hist, source_live)
    target_mass = to_device(target_hist, target_live)
    scaling = to_device(warm_start, target_live)
    tiles = kernel.reshape(N_SRC, PAIRS_DEV, BLK, BLK)
    source_ids = pair_source.reshape(N_SRC, PAIRS_DEV)
    target_ids = pair_target.reshape(N_SRC, PAIRS_DEV)
    block_ids = jnp.arange(SB_DEV, dtype=jnp.int32)
    window_ids = jnp.arange(window_len, dtype=jnp.int32)
    devices = jnp.arange(N_SRC, dtype=jnp.int32)

    def forward(field):
        rounded = lax.optimization_barrier(field.astype(jnp.bfloat16)).astype(jnp.float32)
        spread = rounded.transpose(1, 0, 2, 3).reshape(H, NBS, BLK)
        zero_pad = jnp.zeros((H, RIM, BLK), rounded.dtype)
        padded = jnp.concatenate([zero_pad, spread, zero_pad], axis=1)

        def per_device(device):
            window = lax.dynamic_slice_in_dim(padded, device * SB_DEV, window_len, 1)
            picked = jnp.take(window, target_ids[device], axis=1)
            product = jnp.einsum('hpj,pij->hpi', picked, tiles[device].astype(jnp.float32), precision=lax.Precision.HIGHEST)
            source_pick = (source_ids[device][:, None] == block_ids[None, :]).astype(jnp.float32)
            return jnp.einsum('hpi,ps->hsi', product, source_pick, precision=lax.Precision.HIGHEST)

        return lax.map(per_device, devices)

    def backward(field):
        rounded = lax.optimization_barrier(field.astype(jnp.bfloat16)).astype(jnp.float32)

        def per_device(device):
            picked = jnp.take(rounded[device], source_ids[device], axis=1)
            product = jnp.einsum('hpi,pij->hpj', picked, tiles[device].astype(jnp.float32), precision=lax.Precision.HIGHEST)
            target_pick = (target_ids[device][:, None] == window_ids[None, :]).astype(jnp.float32)
            return jnp.einsum('hpj,pw->hwj', product, target_pick, precision=lax.Precision.HIGHEST)

        partial_win = lax.map(per_device, devices)
        lower_part = partial_win[:, :, :RIM]
        own_part = partial_win[:, :, RIM:RIM + SB_DEV]
        upper_part = partial_win[:, :, RIM + SB_DEV:]
        zero_dev = jnp.zeros((1, H, RIM, BLK), partial_win.dtype)
        from_upper = jnp.concatenate([lower_part[1:], zero_dev], axis=0)
        from_lower = jnp.concatenate([zero_dev, upper_part[:-1]], axis=0)
        own_part = own_part.at[:, :, SB_DEV - RIM:].add(from_upper)
        own_part = own_part.at[:, :, :RIM].add(from_lower)
        return own_part

    source_scale = source_mass
    for sweep in range(ITERS):
        image = forward(scaling)
        source_scale = source_mass / image
        co_image = backward(source_scale)
        scaling = target_mass / co_image
    image = forward(scaling)
    marginal = source_scale * image
    return from_device(scaling).astype(jnp.bfloat16), from_device(marginal).astype(jnp.bfloat16)
```

```python
import functools

import jax
import jax.numpy as jnp
from jax import lax
from jax.experimental import pallas as pl
from jax.experimental.pallas import tpu as pltpu
from jax.sharding import PartitionSpec as P

RIM = 3
ITERS = 2
F32 = jnp.float32
BF16 = jnp.bfloat16
LANES = 128
CHUNKS = 10
UNROLL = 20
GROUP = 1024
F_TILE, F_POS, F_OWN, F_GROUP, F_MAIN, F_RIM, B_TILE, B_BLOCK, B_GROUP, B_LAST = range(10)


def divisor_below(count, most):
    return max(d for d in range(1, most + 1) if count % d == 0)


def build_table(pairs, blocks, pair_src, pair_tgt, stage, table):
    window = blocks + 2 * RIM
    stage[...] = jnp.zeros(stage.shape, jnp.int32)
    stage[0:1, 0:pairs] = pair_src[...]
    stage[1:2, 0:pairs] = pair_tgt[...]
    lane = lax.broadcasted_iota(jnp.int32, (1, LANES), 1)
    used = lane < pairs
    src, tgt = stage[0:1, :], stage[1:2, :]
    outside = (tgt < RIM) | (tgt >= RIM + blocks)
    pad = 4 * GROUP + lane
    key_f = jnp.where(used, jnp.where(outside, GROUP, 0) + src * 32 + tgt, pad).astype(F32)
    key_b = jnp.where(used, jnp.where(outside, 0, GROUP) + tgt * 32 + src, pad).astype(F32)
    place = lax.broadcasted_iota(jnp.int32, (LANES, LANES), 0).astype(F32)
    step = lax.broadcasted_iota(jnp.int32, (LANES, LANES), 1).astype(F32)

    def ordered(key):
        rows = jnp.broadcast_to(key, (LANES, LANES))
        cols = rows.T
        rank = jnp.sum(jnp.where(rows < cols, 1.0, 0.0), axis=1, keepdims=True)
        hit = rank == step
        tile = jnp.sum(jnp.where(hit, place, 0.0), axis=0, keepdims=True)
        code = jnp.sum(jnp.where(hit, cols, 0.0), axis=0, keepdims=True)
        return cols, jnp.clip(tile.astype(jnp.int32), 0, pairs - 1), code.astype(jnp.int32)

    def below(cols, limit):
        count = jnp.sum(jnp.where(cols < limit.astype(F32), 1.0, 0.0), axis=0, keepdims=True)
        return count.astype(jnp.int32)

    def last_or_zero(cols, start):
        low, high = below(cols, start), below(cols, start + 32)
        return jnp.clip(jnp.where(high > low, high - 1, pairs), 0, pairs)

    cols, tile, code = ordered(key_f)
    table[F_TILE : F_TILE + 1, :] = tile
    table[F_POS : F_POS + 1, :] = jnp.clip(code & 31, 0, window - 1)
    table[F_OWN : F_OWN + 1, :] = jnp.clip((code & 31) - RIM, 0, blocks - 1)
    table[F_GROUP : F_GROUP + 1, :] = code >> 5
    table[F_MAIN : F_MAIN + 1, :] = last_or_zero(cols, lane * 32)
    table[F_RIM : F_RIM + 1, :] = last_or_zero(cols, GROUP + lane * 32)
    cols, tile, code = ordered(key_b)
    table[B_TILE : B_TILE + 1, :] = tile
    table[B_BLOCK : B_BLOCK + 1, :] = jnp.clip(code & 31, 0, blocks - 1)
    table[B_GROUP : B_GROUP + 1, :] = code >> 5
    base = jnp.where((lane < RIM) | (lane >= RIM + blocks), 0, GROUP)
    table[B_LAST : B_LAST + 1, :] = last_or_zero(cols, base + lane * 32)


def body(
    n,
    src_cells,
    tgt_cells,
    pair_src,
    pair_tgt,
    kernel_hbm,
    src_hist_hbm,
    tgt_hist_hbm,
    warm_hbm,
    scaling_hbm,
    marginal_hbm,
    tiles,
    tiles_t,
    src_hist,
    tgt_hist,
    warm,
    scaling_out,
    marginal_out,
    stage,
    table,
    tab,
    run,
    own,
    win,
    s_bf,
    s_full,
    term_lo,
    term_hi,
    v_lo,
    v_hi,
    c_lo,
    c_hi,
    local_sem,
    tile_sem,
    send_sem,
    recv_sem,
):
    me = lax.axis_index("src")
    has_lo, has_hi = me > 0, me < n - 1
    pairs, size, _ = tiles.shape
    blocks, hists, _ = s_bf.shape
    rim_steps = RIM * (RIM + 1)
    main_steps = pairs - rim_steps
    chunk = pairs // CHUNKS

    get_warm = pltpu.make_async_copy(warm_hbm, warm, local_sem.at[0])
    get_warm.start()
    get_tiles = []
    for c in range(CHUNKS):
        part = pl.ds(c * chunk, chunk)
        copy = pltpu.make_async_copy(kernel_hbm.at[part], tiles.at[part], tile_sem.at[c])
        copy.start()
        get_tiles.append(copy)
    get_src = pltpu.make_async_copy(src_hist_hbm, src_hist, local_sem.at[1])
    get_src.start()
    get_tgt = pltpu.make_async_copy(tgt_hist_hbm, tgt_hist, local_sem.at[2])
    get_tgt.start()

    barrier = pltpu.get_barrier_semaphore()

    @pl.when(jnp.logical_not(has_lo))
    def _():
        v_lo[...] = jnp.zeros(v_lo.shape, BF16)
        c_lo[...] = jnp.zeros(c_lo.shape, BF16)

    @pl.when(jnp.logical_not(has_hi))
    def _():
        v_hi[...] = jnp.zeros(v_hi.shape, BF16)
        c_hi[...] = jnp.zeros(c_hi.shape, BF16)

    @pl.when(has_lo)
    def _():
        pl.semaphore_signal(barrier, inc=1, device_id={"src": me - 1})

    @pl.when(has_hi)
    def _():
        pl.semaphore_signal(barrier, inc=1, device_id={"src": me + 1})

    build_table(pairs, blocks, pair_src, pair_tgt, stage, table)
    get_tab = pltpu.make_async_copy(table, tab, local_sem.at[3])
    get_tab.start()

    run[pairs] = jnp.zeros((hists, size), F32)

    slot = lax.broadcasted_iota(jnp.int32, (hists, size), 1)

    def masked(ref, cells, b):
        value = ref[:, b * size : (b + 1) * size].astype(F32)
        return jnp.where(slot < cells[b], value, 0.0)

    def copies(index, to_lo, to_hi, at_hi, at_lo):
        down = pltpu.make_async_remote_copy(
            src_ref=to_lo,
            dst_ref=at_hi,
            send_sem=send_sem.at[index, 0],
            recv_sem=recv_sem.at[index, 0],
            device_id={"src": me - 1},
        )
        up = pltpu.make_async_remote_copy(
            src_ref=to_hi,
            dst_ref=at_lo,
            send_sem=send_sem.at[index, 1],
            recv_sem=recv_sem.at[index, 1],
            device_id={"src": me + 1},
        )
        return down, up

    def start(down, up):
        @pl.when(has_lo)
        def _():
            down.start()

        @pl.when(has_hi)
        def _():
            up.start()

    def receive(down, up):
        @pl.when(has_hi)
        def _():
            down.wait_recv()

        @pl.when(has_lo)
        def _():
            up.wait_recv()

    def sent(down, up):
        @pl.when(has_lo)
        def _():
            down.wait_send()

        @pl.when(has_hi)
        def _():
            up.wait_send()

    def steps(low, count, tile_row, field_row, group_row, field, weights, carry):
        unroll = divisor_below(count, UNROLL)

        def some(block, carry):
            acc, before = carry
            for u in range(unroll):
                s = low + block * unroll + u
                group = tab[group_row, s]
                product = jnp.dot(
                    field[tab[field_row, s]],
                    weights[tab[tile_row, s]],
                    preferred_element_type=F32,
                )
                acc = jnp.where(group == before, acc, 0.0) + product
                before = group
                run[s] = acc
            return acc, before

        return lax.fori_loop(0, count // unroll, some, carry)

    def fresh():
        return jnp.zeros((hists, size), F32), jnp.int32(-1)

    edges = list(range(RIM)) + list(range(blocks - RIM, blocks))
    inner = list(range(RIM, blocks - RIM))
    pending = []

    def send_field(k):
        pair = copies(
            k,
            own.at[k, pl.ds(0, RIM)],
            own.at[k, pl.ds(blocks - RIM, RIM)],
            v_hi.at[k],
            v_lo.at[k],
        )
        start(*pair)
        pending.append(pair)
        return pair

    def put_field(k, b, value):
        rounded = value.astype(BF16)
        own[k, b] = rounded
        win[RIM + b] = rounded

    def forward(k, pair):
        carry = steps(0, main_steps, F_TILE, F_OWN, F_GROUP, own.at[k], tiles_t, fresh())
        receive(*pair)
        for r in range(RIM):
            win[r] = v_lo[k, r]
            win[RIM + blocks + r] = v_hi[k, r]
        steps(main_steps, rim_steps, F_TILE, F_POS, F_GROUP, win, tiles_t, carry)

    def image(b):
        return run[tab[F_MAIN, b]] + run[tab[F_RIM, b]]

    get_warm.wait()
    for b in edges:
        put_field(0, b, masked(warm, tgt_cells, b))

    pl.semaphore_wait(barrier, has_lo.astype(jnp.int32) + has_hi.astype(jnp.int32))

    pair = send_field(0)
    for b in inner:
        put_field(0, b, masked(warm, tgt_cells, b))

    for c in range(CHUNKS):
        get_tiles[c].wait()

        def turn(i, carry, c=c):
            tiles_t[c * chunk + i] = tiles[c * chunk + i].T
            return carry

        lax.fori_loop(0, chunk, turn, 0, unroll=divisor_below(chunk, 4))
    get_tab.wait()
    get_src.wait()
    get_tgt.wait()

    put_scaling = pltpu.make_async_copy(scaling_out, scaling_hbm, local_sem.at[4])
    for k in range(ITERS):
        forward(k, pair)
        for b in range(blocks):
            scale = masked(src_hist, src_cells, b) / image(b)
            s_bf[b] = scale.astype(BF16)
            if k == ITERS - 1:
                s_full[b] = scale
        carry = steps(0, rim_steps, B_TILE, B_BLOCK, B_GROUP, s_bf, tiles, fresh())
        for r in range(RIM):
            term_lo[k, r] = run[tab[B_LAST, r]].astype(BF16)
            term_hi[k, r] = run[tab[B_LAST, RIM + blocks + r]].astype(BF16)
        terms = copies(ITERS + 1 + k, term_lo.at[k], term_hi.at[k], c_hi.at[k], c_lo.at[k])
        start(*terms)
        pending.append(terms)
        steps(rim_steps, main_steps, B_TILE, B_BLOCK, B_GROUP, s_bf, tiles, carry)
        receive(*terms)

        def finish(b):
            total = run[tab[B_LAST, RIM + b]]
            if b < RIM:
                total = total + c_lo[k, b].astype(F32)
            if b >= blocks - RIM:
                total = total + c_hi[k, b - (blocks - RIM)].astype(F32)
            value = masked(tgt_hist, tgt_cells, b) / total
            put_field(k + 1, b, value)
            if k == ITERS - 1:
                scaling_out[:, b * size : (b + 1) * size] = value.astype(BF16)

        for b in edges:
            finish(b)
        pair = send_field(k + 1)
        for b in inner:
            finish(b)
    put_scaling.start()
    forward(ITERS, pair)
    for b in range(blocks):
        marginal_out[:, b * size : (b + 1) * size] = (s_full[b] * image(b)).astype(BF16)
    put_marginal = pltpu.make_async_copy(marginal_out, marginal_hbm, local_sem.at[5])
    put_marginal.start()
    for pair in pending:
        sent(*pair)
    put_scaling.wait()
    put_marginal.wait()


def local(
    kernel,
    pair_source,
    pair_target,
    source_cells,
    target_cells,
    source_hist,
    target_hist,
    warm_start,
):
    pairs, size, _ = kernel.shape
    blocks = source_cells.shape[0]
    hists = source_hist.shape[0]
    window = blocks + 2 * RIM
    n = lax.axis_size("src")
    exchanges = 2 * ITERS + 1
    flat = source_hist.shape
    smem = pl.BlockSpec(memory_space=pltpu.SMEM)
    vmem = pl.BlockSpec(memory_space=pltpu.VMEM)
    hbm = pl.BlockSpec(memory_space=pl.ANY)
    field = (blocks, hists, size)
    rim = (RIM, hists, size)
    return pl.pallas_call(
        functools.partial(body, n),
        out_shape=(jax.ShapeDtypeStruct(flat, BF16), jax.ShapeDtypeStruct(flat, BF16)),
        in_specs=[smem, smem, vmem, vmem, hbm, hbm, hbm, hbm],
        out_specs=(hbm, hbm),
        scratch_shapes=[
            pltpu.VMEM(kernel.shape, BF16),
            pltpu.VMEM(kernel.shape, BF16),
            pltpu.VMEM(flat, BF16),
            pltpu.VMEM(flat, BF16),
            pltpu.VMEM(flat, BF16),
            pltpu.VMEM(flat, BF16),
            pltpu.VMEM(flat, BF16),
            pltpu.VMEM((8, LANES), jnp.int32),
            pltpu.VMEM((16, LANES), jnp.int32),
            pltpu.SMEM((16, LANES), jnp.int32),
            pltpu.VMEM((pairs + 1, hists, size), F32),
            pltpu.VMEM((ITERS + 1,) + field, BF16),
            pltpu.VMEM((window, hists, size), BF16),
            pltpu.VMEM(field, BF16),
            pltpu.VMEM(field, F32),
            pltpu.VMEM((ITERS,) + rim, BF16),
            pltpu.VMEM((ITERS,) + rim, BF16),
            pltpu.VMEM((ITERS + 1,) + rim, BF16),
            pltpu.VMEM((ITERS + 1,) + rim, BF16),
            pltpu.VMEM((ITERS,) + rim, BF16),
            pltpu.VMEM((ITERS,) + rim, BF16),
            pltpu.SemaphoreType.DMA((6,)),
            pltpu.SemaphoreType.DMA((CHUNKS,)),
            pltpu.SemaphoreType.DMA((exchanges, 2)),
            pltpu.SemaphoreType.DMA((exchanges, 2)),
        ],
        compiler_params=pltpu.CompilerParams(
            collective_id=0, has_side_effects=True, vmem_limit_bytes=52 * 2**20
        ),
    )(
        source_cells,
        target_cells,
        pair_source.reshape(1, pairs),
        pair_target.reshape(1, pairs),
        kernel,
        source_hist,
        target_hist,
        warm_start,
    )


def solution(mesh):
    in_specs = (
        P(("grp", "src"), None, None),
        P(("grp", "src")),
        P(("grp", "src")),
        P(("grp", "src")),
        P(("grp", "src")),
        P(None, ("grp", "src")),
        P(None, ("grp", "src")),
        P(None, ("grp", "src")),
    )
    out_specs = (P(None, ("grp", "src")), P(None, ("grp", "src")))
    return jax.shard_map(local, mesh=mesh, in_specs=in_specs, out_specs=out_specs, check_vma=False)
```

```python
import functools

import jax
import jax.numpy as jnp
from jax import lax
from jax.experimental import pallas as pl
from jax.experimental.pallas import tpu as pltpu
from jax.sharding import PartitionSpec as P

RIM = 3
ITERS = 2
F32 = jnp.float32
BF16 = jnp.bfloat16
LANES = 128
CHUNKS = 10
UNROLL = 34
GROUP = 1024
F_TILE, F_POS, F_OWN, F_GROUP, F_MAIN, F_RIM, B_TILE, B_BLOCK, B_GROUP, B_LAST = range(10)


def divisor_below(count, most):
    return max(d for d in range(1, most + 1) if count % d == 0)


def build_table(pairs, blocks, pair_src, pair_tgt, stage, table):
    window = blocks + 2 * RIM
    stage[...] = jnp.zeros(stage.shape, jnp.int32)
    stage[0:1, 0:pairs] = pair_src[...]
    stage[1:2, 0:pairs] = pair_tgt[...]
    lane = lax.broadcasted_iota(jnp.int32, (1, LANES), 1)
    used = lane < pairs
    src, tgt = stage[0:1, :], stage[1:2, :]
    outside = (tgt < RIM) | (tgt >= RIM + blocks)
    pad = 4 * GROUP + lane
    key_f = jnp.where(used, jnp.where(outside, GROUP, 0) + src * 32 + tgt, pad).astype(F32)
    key_b = jnp.where(used, jnp.where(outside, 0, GROUP) + tgt * 32 + src, pad).astype(F32)
    place = lax.broadcasted_iota(jnp.int32, (LANES, LANES), 0).astype(F32)
    step = lax.broadcasted_iota(jnp.int32, (LANES, LANES), 1).astype(F32)

    def ordered(key):
        rows = jnp.broadcast_to(key, (LANES, LANES))
        cols = rows.T
        rank = jnp.sum(jnp.where(rows < cols, 1.0, 0.0), axis=1, keepdims=True)
        hit = rank == step
        tile = jnp.sum(jnp.where(hit, place, 0.0), axis=0, keepdims=True)
        code = jnp.sum(jnp.where(hit, cols, 0.0), axis=0, keepdims=True)
        return cols, jnp.clip(tile.astype(jnp.int32), 0, pairs - 1), code.astype(jnp.int32)

    def below(cols, limit):
        count = jnp.sum(jnp.where(cols < limit.astype(F32), 1.0, 0.0), axis=0, keepdims=True)
        return count.astype(jnp.int32)

    def last_or_zero(cols, start):
        low, high = below(cols, start), below(cols, start + 32)
        return jnp.clip(jnp.where(high > low, high - 1, pairs), 0, pairs)

    cols, tile, code = ordered(key_f)
    table[F_TILE : F_TILE + 1, :] = tile
    table[F_POS : F_POS + 1, :] = jnp.clip(code & 31, 0, window - 1)
    table[F_OWN : F_OWN + 1, :] = jnp.clip((code & 31) - RIM, 0, blocks - 1)
    table[F_GROUP : F_GROUP + 1, :] = code >> 5
    table[F_MAIN : F_MAIN + 1, :] = last_or_zero(cols, lane * 32)
    table[F_RIM : F_RIM + 1, :] = last_or_zero(cols, GROUP + lane * 32)
    cols, tile, code = ordered(key_b)
    table[B_TILE : B_TILE + 1, :] = tile
    table[B_BLOCK : B_BLOCK + 1, :] = jnp.clip(code & 31, 0, blocks - 1)
    table[B_GROUP : B_GROUP + 1, :] = code >> 5
    base = jnp.where((lane < RIM) | (lane >= RIM + blocks), 0, GROUP)
    table[B_LAST : B_LAST + 1, :] = last_or_zero(cols, base + lane * 32)


def body(
    n,
    src_cells_hbm,
    tgt_cells_hbm,
    pair_src_hbm,
    pair_tgt_hbm,
    kernel_hbm,
    src_hist_hbm,
    tgt_hist_hbm,
    warm_hbm,
    scaling_hbm,
    marginal_hbm,
    src_cells,
    tgt_cells,
    pair_src,
    pair_tgt,
    tiles,
    tiles_t,
    src_hist,
    tgt_hist,
    warm,
    scaling_out,
    marginal_out,
    stage,
    table,
    tab,
    run,
    own,
    win,
    s_bf,
    s_full,
    term_lo,
    term_hi,
    v_lo,
    v_hi,
    c_lo,
    c_hi,
    local_sem,
    tile_sem,
    send_sem,
    recv_sem,
):
    me = lax.axis_index("src")
    has_lo, has_hi = me > 0, me < n - 1
    pairs, size, _ = tiles.shape
    blocks, hists, _ = s_bf.shape
    rim_steps = RIM * (RIM + 1)
    main_steps = pairs - rim_steps
    chunk = pairs // CHUNKS

    small = []
    for i, (ref, held) in enumerate(
        (
            (pair_src_hbm, pair_src),
            (pair_tgt_hbm, pair_tgt),
            (tgt_cells_hbm, tgt_cells),
            (src_cells_hbm, src_cells),
        )
    ):
        copy = pltpu.make_async_copy(ref, held, local_sem.at[6 + i])
        copy.start()
        small.append(copy)
    get_warm = pltpu.make_async_copy(warm_hbm, warm, local_sem.at[0])
    get_warm.start()
    get_tiles = []
    for c in range(CHUNKS):
        part = pl.ds(c * chunk, chunk)
        copy = pltpu.make_async_copy(kernel_hbm.at[part], tiles.at[part], tile_sem.at[c])
        copy.start()
        get_tiles.append(copy)
    get_src = pltpu.make_async_copy(src_hist_hbm, src_hist, local_sem.at[1])
    get_src.start()
    get_tgt = pltpu.make_async_copy(tgt_hist_hbm, tgt_hist, local_sem.at[2])
    get_tgt.start()

    barrier = pltpu.get_barrier_semaphore()

    @pl.when(jnp.logical_not(has_lo))
    def _():
        v_lo[...] = jnp.zeros(v_lo.shape, BF16)
        c_lo[...] = jnp.zeros(c_lo.shape, BF16)

    @pl.when(jnp.logical_not(has_hi))
    def _():
        v_hi[...] = jnp.zeros(v_hi.shape, BF16)
        c_hi[...] = jnp.zeros(c_hi.shape, BF16)

    @pl.when(has_lo)
    def _():
        pl.semaphore_signal(barrier, inc=1, device_id={"src": me - 1})

    @pl.when(has_hi)
    def _():
        pl.semaphore_signal(barrier, inc=1, device_id={"src": me + 1})

    small[0].wait()
    small[1].wait()
    build_table(pairs, blocks, pair_src, pair_tgt, stage, table)
    get_tab = pltpu.make_async_copy(table, tab, local_sem.at[3])
    get_tab.start()

    run[pairs] = jnp.zeros((hists, size), F32)

    slot = lax.broadcasted_iota(jnp.int32, (hists, size), 1)

    def masked(ref, cells, b):
        value = ref[:, b * size : (b + 1) * size].astype(F32)
        return jnp.where(slot < cells[b], value, 0.0)

    def copies(index, to_lo, to_hi, at_hi, at_lo):
        down = pltpu.make_async_remote_copy(
            src_ref=to_lo,
            dst_ref=at_hi,
            send_sem=send_sem.at[index, 0],
            recv_sem=recv_sem.at[index, 0],
            device_id={"src": me - 1},
        )
        up = pltpu.make_async_remote_copy(
            src_ref=to_hi,
            dst_ref=at_lo,
            send_sem=send_sem.at[index, 1],
            recv_sem=recv_sem.at[index, 1],
            device_id={"src": me + 1},
        )
        return down, up

    def start(down, up):
        @pl.when(has_lo)
        def _():
            down.start()

        @pl.when(has_hi)
        def _():
            up.start()

    def receive(down, up):
        @pl.when(has_hi)
        def _():
            down.wait_recv()

        @pl.when(has_lo)
        def _():
            up.wait_recv()

    def sent(down, up):
        @pl.when(has_lo)
        def _():
            down.wait_send()

        @pl.when(has_hi)
        def _():
            up.wait_send()

    def steps(low, count, tile_row, field_row, group_row, field, carry, turning=False):
        unroll = divisor_below(count, UNROLL)

        def some(block, carry):
            acc, before = carry
            for u in range(unroll):
                s = low + block * unroll + u
                group = tab[group_row, s]
                if turning:
                    tile = tiles[tab[tile_row, s]].T
                    tiles_t[s] = tile
                elif tile_row == F_TILE:
                    tile = tiles_t[s]
                else:
                    tile = tiles[tab[tile_row, s]]
                product = jnp.dot(
                    field[tab[field_row, s]],
                    tile,
                    preferred_element_type=F32,
                )
                acc = jnp.where(group == before, acc, 0.0) + product
                before = group
                run[s] = acc
            return acc, before

        return lax.fori_loop(0, count // unroll, some, carry)

    def fresh():
        return jnp.zeros((hists, size), F32), jnp.int32(-1)

    edges = list(range(RIM)) + list(range(blocks - RIM, blocks))
    inner = list(range(RIM, blocks - RIM))
    pending = []

    def send_field(k):
        pair = copies(
            k,
            own.at[k, pl.ds(0, RIM)],
            own.at[k, pl.ds(blocks - RIM, RIM)],
            v_hi.at[k],
            v_lo.at[k],
        )
        start(*pair)
        pending.append(pair)
        return pair

    def put_field(k, b, value):
        rounded = value.astype(BF16)
        own[k, b] = rounded
        win[RIM + b] = rounded

    def forward(k, pair):
        carry = steps(0, main_steps, F_TILE, F_OWN, F_GROUP, own.at[k], fresh(), k == 0)
        receive(*pair)
        for r in range(RIM):
            win[r] = v_lo[k, r]
            win[RIM + blocks + r] = v_hi[k, r]
        steps(main_steps, rim_steps, F_TILE, F_POS, F_GROUP, win, carry, k == 0)

    def image(b):
        return run[tab[F_MAIN, b]] + run[tab[F_RIM, b]]

    get_warm.wait()
    small[2].wait()
    small[3].wait()
    for b in edges:
        put_field(0, b, masked(warm, tgt_cells, b))

    pl.semaphore_wait(barrier, has_lo.astype(jnp.int32) + has_hi.astype(jnp.int32))

    pair = send_field(0)
    for b in inner:
        put_field(0, b, masked(warm, tgt_cells, b))

    for c in range(CHUNKS):
        get_tiles[c].wait()
    get_tab.wait()
    get_src.wait()
    get_tgt.wait()

    put_scaling = pltpu.make_async_copy(scaling_out, scaling_hbm, local_sem.at[4])
    for k in range(ITERS):
        forward(k, pair)
        for b in range(blocks):
            scale = masked(src_hist, src_cells, b) / image(b)
            s_bf[b] = scale.astype(BF16)
            if k == ITERS - 1:
                s_full[b] = scale
        carry = steps(0, rim_steps, B_TILE, B_BLOCK, B_GROUP, s_bf, fresh())
        for r in range(RIM):
            term_lo[k, r] = run[tab[B_LAST, r]].astype(BF16)
            term_hi[k, r] = run[tab[B_LAST, RIM + blocks + r]].astype(BF16)
        terms = copies(ITERS + 1 + k, term_lo.at[k], term_hi.at[k], c_hi.at[k], c_lo.at[k])
        start(*terms)
        pending.append(terms)
        steps(rim_steps, main_steps, B_TILE, B_BLOCK, B_GROUP, s_bf, carry)
        receive(*terms)

        def finish(b):
            total = run[tab[B_LAST, RIM + b]]
            if b < RIM:
                total = total + c_lo[k, b].astype(F32)
            if b >= blocks - RIM:
                total = total + c_hi[k, b - (blocks - RIM)].astype(F32)
            value = masked(tgt_hist, tgt_cells, b) / total
            put_field(k + 1, b, value)
            if k == ITERS - 1:
                scaling_out[:, b * size : (b + 1) * size] = value.astype(BF16)

        for b in edges:
            finish(b)
        pair = send_field(k + 1)
        for b in inner:
            finish(b)
    put_scaling.start()
    forward(ITERS, pair)
    for b in range(blocks):
        marginal_out[:, b * size : (b + 1) * size] = (s_full[b] * image(b)).astype(BF16)
    put_marginal = pltpu.make_async_copy(marginal_out, marginal_hbm, local_sem.at[5])
    put_marginal.start()
    for pair in pending:
        sent(*pair)
    put_scaling.wait()
    put_marginal.wait()


def local(
    kernel,
    pair_source,
    pair_target,
    source_cells,
    target_cells,
    source_hist,
    target_hist,
    warm_start,
):
    pairs, size, _ = kernel.shape
    blocks = source_cells.shape[0]
    hists = source_hist.shape[0]
    window = blocks + 2 * RIM
    n = lax.axis_size("src")
    exchanges = 2 * ITERS + 1
    flat = source_hist.shape
    hbm = pl.BlockSpec(memory_space=pl.ANY)
    field = (blocks, hists, size)
    rim = (RIM, hists, size)
    return pl.pallas_call(
        functools.partial(body, n),
        out_shape=(jax.ShapeDtypeStruct(flat, BF16), jax.ShapeDtypeStruct(flat, BF16)),
        in_specs=[hbm] * 8,
        out_specs=(hbm, hbm),
        scratch_shapes=[
            pltpu.SMEM(source_cells.shape, jnp.int32),
            pltpu.SMEM(target_cells.shape, jnp.int32),
            pltpu.VMEM((1, pairs), jnp.int32),
            pltpu.VMEM((1, pairs), jnp.int32),
            pltpu.VMEM(kernel.shape, BF16),
            pltpu.VMEM(kernel.shape, BF16),
            pltpu.VMEM(flat, BF16),
            pltpu.VMEM(flat, BF16),
            pltpu.VMEM(flat, BF16),
            pltpu.VMEM(flat, BF16),
            pltpu.VMEM(flat, BF16),
            pltpu.VMEM((8, LANES), jnp.int32),
            pltpu.VMEM((16, LANES), jnp.int32),
            pltpu.SMEM((16, LANES), jnp.int32),
            pltpu.VMEM((pairs + 1, hists, size), F32),
            pltpu.VMEM((ITERS + 1,) + field, BF16),
            pltpu.VMEM((window, hists, size), BF16),
            pltpu.VMEM(field, BF16),
            pltpu.VMEM(field, F32),
            pltpu.VMEM((ITERS,) + rim, BF16),
            pltpu.VMEM((ITERS,) + rim, BF16),
            pltpu.VMEM((ITERS + 1,) + rim, BF16),
            pltpu.VMEM((ITERS + 1,) + rim, BF16),
            pltpu.VMEM((ITERS,) + rim, BF16),
            pltpu.VMEM((ITERS,) + rim, BF16),
            pltpu.SemaphoreType.DMA((10,)),
            pltpu.SemaphoreType.DMA((CHUNKS,)),
            pltpu.SemaphoreType.DMA((exchanges, 2)),
            pltpu.SemaphoreType.DMA((exchanges, 2)),
        ],
        compiler_params=pltpu.CompilerParams(
            collective_id=0, has_side_effects=True, vmem_limit_bytes=62 * 2**20
        ),
    )(
        source_cells,
        target_cells,
        pair_source.reshape(1, pairs),
        pair_target.reshape(1, pairs),
        kernel,
        source_hist,
        target_hist,
        warm_start,
    )


def solution(mesh):
    in_specs = (
        P(("grp", "src"), None, None),
        P(("grp", "src")),
        P(("grp", "src")),
        P(("grp", "src")),
        P(("grp", "src")),
        P(None, ("grp", "src")),
        P(None, ("grp", "src")),
        P(None, ("grp", "src")),
    )
    out_specs = (P(None, ("grp", "src")), P(None, ("grp", "src")))
    return jax.shard_map(local, mesh=mesh, in_specs=in_specs, out_specs=out_specs, check_vma=False)
```
